32 devices in a mesh: rep: 8 (over z, x), grp: 4 (over y, core).
Axes of the slice: x: 2, y: 2, z: 4, core: 2. Of those that a mesh axis runs over, the one named last changes fastest.
Arguments:
- inputs: bfloat16 [2, 65536, 1152], P(None, ('rep', 'grp')), may hold values from -6 to 6
- out_grads: bfloat16 [2, 65536, 1152], P(None, ('rep', 'grp')), may hold values from -6 to 6
- weights: bfloat16 [2, 1152, 1152], P(None, 'grp'), may hold values from -3 to 3
- biases: bfloat16 [2, 1152], P(None, 'grp'), may hold values from -3 to 3
- errors: float32 [8, 2, 1152, 1152], P('rep', None, 'grp'), may hold values from -6 to 6
- momenta: float32 [2, 1152, 1152], P(None, 'grp'), may hold values from -3 to 3
- bias_momenta: float32 [2, 1152], P(None, 'grp'), may hold values from -3 to 3
- q_start: float32 [2, 1152, 32], replicated, may hold values from -6 to 6
Outputs:
- new_weights: bfloat16 [2, 1152, 1152], replicated
- new_biases: bfloat16 [2, 1152], replicated
- new_errors: float32 [8, 2, 1152, 1152], P('rep', None, 'grp')
- new_momenta: float32 [2, 1152, 1152], P(None, 'grp')
- new_bias_momenta: float32 [2, 1152], P(None, 'grp')
The draws below stay inside these ranges and needn't reach their ends.
All inputs are finite; a program needn't handle non-finite values.
Results may differ from the reference program's by a relative error of at most 0.0045.
Values may be sent and summed in bfloat16 or wider, within the bound.
A program may use at most 256 MiB of HBM per device.

```python
import jax
import jax.numpy as jnp
from jax import lax

D = 1152
RANK = 32
LAYERS = 2
ROUNDS = 2
NS_STEPS = 5
TOK_DEV = 2048
REPS = 8
TOKENS = 65536
N_GRP = 4


def steps_of(rng, dims, cuts, low, top_value):
    factor_of, own = 1.0, jax.random.fold_in(rng, 6)
    for dim, blocks in cuts:
        heights = jnp.exp(jax.random.uniform(jax.random.fold_in(own, dim), (blocks,), jnp.float32, low / len(cuts), top_value / len(cuts)))
        factor_of = factor_of * jnp.repeat(heights, dims[dim] // blocks).reshape([-1 if axis == dim else 1 for axis in range(len(dims))])
    return factor_of


def gaussian(rng, extent, width, reach, pieces=(), kind=jnp.bfloat16):
    result = jax.random.normal(rng, extent, jnp.float32) * width
    if len(pieces) > 0:
        result = steps_of(rng, extent, pieces, -0.22, 0.18) * result
    return jnp.clip(result, min=-reach, max=reach).astype(kind)


def setup_inputs(seed: int = 0) -> dict:
    streams_of = jax.random.split(jax.random.key(seed), 9)
    return {
        "inputs": gaussian(streams_of[0], (LAYERS, TOKENS, D), 1.0, 6.0, ((1, 32),)),
        "out_grads": gaussian(streams_of[1], (LAYERS, TOKENS, D), 1.0, 6.0, ((1, 32),)),
        "weights": gaussian(streams_of[2], (LAYERS, D, D), 0.5, 3.0, ((1, 4),)),
        "biases": gaussian(streams_of[3], (LAYERS, D), 0.5, 3.0, ((1, 4),)),
        "errors": gaussian(streams_of[4], (REPS, LAYERS, D, D), 1.0, 6.0, ((0, 8), (2, 4)), jnp.float32),
        "momenta": gaussian(streams_of[5], (LAYERS, D, D), 0.5, 3.0, ((1, 4),), jnp.float32),
        "bias_momenta": gaussian(streams_of[6], (LAYERS, D), 0.5, 3.0, ((1, 4),), jnp.float32),
        "q_start": gaussian(streams_of[7], (LAYERS, D, RANK), 1.0, 6.0, (), jnp.float32),
    }


HIGH = lax.Precision.HIGHEST

def orthonormal(p_sum, gram):
    fro = jnp.sqrt(lax.optimization_barrier(jnp.sum(gram * gram, axis=(1, 2)))) + 1e-06
    scaled = gram / fro[:, None, None]
    eye = jnp.eye(gram.shape[-1], dtype=jnp.float32)
    ymat = scaled
    zmat = jnp.broadcast_to(eye, gram.shape)
    for step in range(NS_STEPS):
        tmat = 1.5 * eye - 0.5 * jnp.einsum('lab,lbc->lac', zmat, ymat, precision=HIGH)
        ymat = jnp.einsum('lab,lbc->lac', ymat, tmat, precision=HIGH)
        zmat = jnp.einsum('lab,lbc->lac', tmat, zmat, precision=HIGH)
    phat = jnp.einsum('lrk,lkj->lrj', p_sum, zmat, precision=HIGH)
    return phat / jnp.sqrt(fro)[:, None, None]

def reference(inputs, out_grads, weights, biases, errors, momenta, bias_momenta, q_start):
    rep_tok = TOK_DEV * N_GRP
    scale = float(TOK_DEV) ** (-0.5)

    def replica(index):
        start = (index * rep_tok).astype(jnp.int32)
        xs = lax.dynamic_slice_in_dim(inputs, start, rep_tok, 1)
        ys = lax.dynamic_slice_in_dim(out_grads, start, rep_tok, 1)
        grads = [jnp.dot(xs[l].T, ys[l], preferred_element_type=jnp.float32) for l in range(LAYERS)]
        return jnp.stack(grads) * scale
    grad = lax.map(replica, jnp.arange(REPS, dtype=jnp.int32))
    merged = grad + errors
    bias_grad = lax.optimization_barrier(jnp.sum(out_grads, axis=1, dtype=jnp.float32)) * (scale / REPS)
    qmat = q_start
    phat = None
    for rnd in range(ROUNDS):
        p_sum = jnp.einsum('xlde,lek->ldk', merged, qmat, precision=HIGH)
        gram = jnp.einsum('ldk,ldj->lkj', p_sum, p_sum, precision=HIGH)
        phat = orthonormal(p_sum, gram)
        qmat = jnp.einsum('xlde,ldk->lek', merged, phat, precision=HIGH)
    approx = jnp.einsum('ldk,lek->lde', phat, qmat, precision=HIGH) / REPS
    new_errors = merged - approx[None]
    new_momenta = 0.9 * momenta + approx
    new_weights = (weights.astype(jnp.float32) - 0.5 * new_momenta).astype(jnp.bfloat16)
    new_bias_momenta = 0.9 * bias_momenta + bias_grad
    new_biases = (biases.astype(jnp.float32) - 0.5 * new_bias_momenta).astype(jnp.bfloat16)
    return (new_weights, new_biases, new_errors, new_momenta, new_bias_momenta)
```

```python
import functools

import jax
import jax.numpy as jnp
from jax import lax
from jax.experimental import pallas as pl
from jax.experimental.pallas import tpu as pltpu
from jax.sharding import PartitionSpec as P

ROUNDS = 2
NS_STEPS = 5
HIGH = lax.Precision.HIGHEST
F32 = jnp.float32
BF16 = jnp.bfloat16
NN = (((1,), (0,)), ((), ()))
NT = (((1,), (1,)), ((), ()))
TN = (((0,), (0,)), ((), ()))


def dot(a, b, dims, precision=None):
    return lax.dot_general(a, b, dims, precision=precision, preferred_element_type=F32)


def split(a):
    hi = a.astype(BF16)
    return hi, (a - hi.astype(F32)).astype(BF16)


def step_kernel(sizes, x_hbm, y_hbm, errors, weights, momenta, q0, bias_in,
                merged, phat_out, q_out, w_out, bias_out, small_out,
                xbuf, ybuf, gfull, gsend, grecv, ysend, yrecv, mhi, mlo, wown,
                psend, prs, pfull, tsend, trs, tmid, trr, tag, brep, bgrp, bsmall,
                load_sem, s_core, r_core, s_y, r_y, s_wc, r_wc, s_rep, r_rep, s_grp, r_grp):
    L, G, R, rank, width, tok, chunk = sizes
    rows = width // G
    K = L * rank
    Y = G // 2
    pp = psend.shape[2]
    pr = tsend.shape[3]
    scale = float(tok) ** (-0.5)
    me_r = lax.axis_index("rep")
    me_g = lax.axis_index("grp")
    core = lax.rem(me_g, 2)
    yy = lax.div(me_g, 2)
    mate = me_g + 1 - 2 * core

    loads = []
    for l in range(L):
        for which, (src, dst) in enumerate(((x_hbm, xbuf), (y_hbm, ybuf))):
            loads.append(pltpu.make_async_copy(src.at[l], dst.at[l], load_sem.at[2 * l + which]))
            loads[-1].start()

    barrier = pltpu.get_barrier_semaphore()
    for d in range(1, R):
        pl.semaphore_signal(barrier, inc=1, device_id={"rep": lax.rem(me_r + d, R)},
                            device_id_type=pl.DeviceIdType.MESH)
    for d in range(1, G):
        pl.semaphore_signal(barrier, inc=1, device_id={"grp": lax.rem(me_g + d, G)},
                            device_id_type=pl.DeviceIdType.MESH)
    pl.semaphore_wait(barrier, R + G - 2)

    def remote(src, dst, send, recv, axis, peer):
        copy = pltpu.make_async_remote_copy(
            src_ref=src, dst_ref=dst, send_sem=send, recv_sem=recv,
            device_id={axis: peer}, device_id_type=pl.DeviceIdType.MESH)
        copy.start()
        return copy

    def over_rep(phase, src, dst):
        return [remote(src(lax.rem(me_r + d, R)), dst, s_rep.at[phase, d - 1], r_rep.at[phase, d - 1],
                       "rep", lax.rem(me_r + d, R)) for d in range(1, R)]

    def over_grp(phase, src, dst):
        return [remote(src(lax.rem(me_g + d, G)), dst, s_grp.at[phase, d - 1], r_grp.at[phase, d - 1],
                       "grp", lax.rem(me_g + d, G)) for d in range(1, G)]

    def wait(copies):
        for copy in copies:
            copy.wait_recv()
        for copy in copies:
            copy.wait_send()

    def row_ds(g):
        return pl.ds(pl.multiple_of(g * rows, 16), rows)

    bsmall[me_g] = bias_in[...]
    small_copies = over_grp(0, lambda g: bsmall.at[me_g], bsmall.at[me_g])

    def grads(l):
        loads[2 * l].wait()
        loads[2 * l + 1].wait()

        def one(j, carry):
            at = pl.ds(pl.multiple_of(j * chunk, 128), chunk)
            gfull[l, at, :] = dot(xbuf[l, :, at], ybuf[l], TN)
            return carry

        lax.fori_loop(0, width // chunk, one, 0)
        for y in range(Y):
            gsend[l, y] = gfull[l, row_ds(2 * y + 1 - core), :].astype(BF16)
        return remote(gsend.at[l], grecv.at[l], s_core.at[l], r_core.at[l], "grp", mate)

    def to_y(l, core_copy):
        core_copy.wait_recv()
        copies = []
        for d in range(1, Y):
            y = lax.rem(yy + d, Y)
            ysend[l, d - 1] = (gfull[l, row_ds(2 * y + core), :] + grecv[l, y].astype(F32)).astype(BF16)
            copies.append(remote(ysend.at[l, d - 1], yrecv.at[l, d - 1], s_y.at[l, d - 1],
                                 r_y.at[l, d - 1], "grp", 2 * y + core))
        return copies

    core_copies, y_copies = [], []
    for l in range(L):
        core_copies.append(grads(l))
        if l > 0:
            y_copies.append(to_y(l - 1, core_copies[l - 1]))
    for l in range(L):
        total = dot(jnp.ones((8, tok), BF16), ybuf[l], NN)
        brep[me_r, pl.ds(l, 1), :] = total[:1]
    bias_copies = over_rep(0, lambda r: brep.at[me_r], brep.at[me_r])
    y_copies.append(to_y(L - 1, core_copies[L - 1]))
    for l in range(L):
        wown[l] = (weights[l].astype(F32) - 0.45 * momenta[l]).astype(BF16)
    wait(bias_copies)
    bgrp[me_g] = jnp.sum(brep[...], axis=0)
    bias_copies = over_grp(1, lambda g: bgrp.at[me_g], bgrp.at[me_g])
    local_w = pltpu.make_async_copy(wown, w_out.at[me_g], load_sem.at[2 * L])
    local_w.start()
    for l in range(L):
        for copy in y_copies[l]:
            copy.wait_recv()
        total = gfull[l, row_ds(me_g), :] + grecv[l, yy].astype(F32)
        for d in range(1, Y):
            total = total + yrecv[l, d - 1].astype(F32)
        m = total * scale + errors[l]
        merged[l] = m
        hi, lo = split(m)
        mhi[l] = hi
        mlo[l] = lo
    w_copies = [remote(wown, w_out.at[me_g], s_wc.at[d - 1], r_wc.at[d - 1], "grp",
                       lax.rem(me_g + d, G)) for d in range(1, G)]

    def apply(a, l, dims):
        hi, lo = split(a)
        both = dot(jnp.concatenate([hi, lo], axis=0), mhi[l], dims)
        return both[:rank] + both[rank:] + dot(hi, mlo[l], dims)

    row = lax.broadcasted_iota(jnp.int32, (K, K), 0)
    col = lax.broadcasted_iota(jnp.int32, (K, K), 1)
    same = (lax.div(row, rank) == lax.div(col, rank)).astype(F32)
    eye = (row == col).astype(F32)
    layer_of = lax.div(lax.broadcasted_iota(jnp.int32, (K, 1), 0), rank)

    q = [q0[l] for l in range(L)]
    for rnd in range(ROUNDS):
        p = jnp.concatenate([apply(q[l], l, NT) for l in range(L)], axis=0)
        for r in range(R):
            if r * pp < K:
                psend[rnd, r] = p[r * pp:(r + 1) * pp]
        prs[rnd, me_r] = psend[rnd, me_r]
        wait(over_rep(1 + 4 * rnd, lambda r: psend.at[rnd, r], prs.at[rnd, me_r]))
        pfull[rnd, me_g, me_r] = jnp.sum(prs[rnd], axis=0)
        wait(over_rep(2 + 4 * rnd, lambda r: pfull.at[rnd, me_g, me_r], pfull.at[rnd, me_g, me_r]))
        p_copies = over_grp(2 + 3 * rnd, lambda g: pfull.at[rnd, me_g], pfull.at[rnd, me_g])

        def whole_p(g):
            return jnp.concatenate([pfull[rnd, g, r] for r in range(R)], axis=0)[:K]

        p = whole_p(me_g)
        t = jnp.concatenate([apply(p[l * rank:(l + 1) * rank], l, NN) for l in range(L)], axis=0)
        for i in range(G * R):
            if i * pr < K:
                tsend[rnd, i // R, i % R] = t[i * pr:(i + 1) * pr]
        trs[rnd, me_g] = tsend[rnd, me_g]
        copies = over_grp(3 + 3 * rnd, lambda g: tsend.at[rnd, g], trs.at[rnd, me_g])

        wait(p_copies)
        gram = jnp.zeros((K, K), F32)
        for g in range(G):
            pg = whole_p(g)
            gram = gram + dot(pg, pg, NT, HIGH)
        gram = gram * same
        squares = jnp.sum(gram * gram, axis=1, keepdims=True)
        fro = jnp.zeros((K, 1), F32)
        for l in range(L):
            mine = layer_of == l
            one = jnp.sum(jnp.where(mine, squares, 0.0), axis=0, keepdims=True)
            fro = jnp.where(mine, jnp.sqrt(one) + 1e-06, fro)
        ymat, zmat = gram / fro, eye

        def newton(ymat, zmat, count):
            for _ in range(count):
                tmat = 1.5 * eye - 0.5 * dot(zmat, ymat, NN, HIGH)
                ymat = dot(ymat, tmat, NN, HIGH)
                zmat = dot(tmat, zmat, NN, HIGH)
            return ymat, zmat

        ymat, zmat = newton(ymat, zmat, 1)
        wait(copies)
        tmid[rnd] = jnp.sum(trs[rnd], axis=0)
        trr[rnd, me_r] = tmid[rnd, me_r]
        copies = over_rep(3 + 4 * rnd, lambda r: tmid.at[rnd, r], trr.at[rnd, me_r])
        ymat, zmat = newton(ymat, zmat, 2)
        wait(copies)
        tag[rnd, me_g, me_r] = jnp.sum(trr[rnd], axis=0)
        copies = over_rep(4 + 4 * rnd, lambda r: tag.at[rnd, me_g, me_r], tag.at[rnd, me_g, me_r])
        ymat, zmat = newton(ymat, zmat, NS_STEPS - 3)
        wait(copies)
        wait(over_grp(4 + 3 * rnd, lambda g: tag.at[rnd, me_g], tag.at[rnd, me_g]))
        t = jnp.concatenate([tag[rnd, i // R, i % R] for i in range(G * R)], axis=0)[:K]
        inv = 1.0 / jnp.sqrt(fro)
        qall = dot(zmat, t, TN, HIGH) * inv
        q = [qall[l * rank:(l + 1) * rank] for l in range(L)]
        if rnd == ROUNDS - 1:
            q_out[...] = qall
            for g in range(G):
                phat_out[g] = dot(zmat, whole_p(g), TN, HIGH) * inv

    wait(bias_copies)
    wait(small_copies)
    bias_out[...] = jnp.sum(bgrp[...], axis=0)
    small_out[...] = bsmall[...]
    for l in range(L):
        core_copies[l].wait_send()
        for copy in y_copies[l]:
            copy.wait_send()
    local_w.wait()
    wait(w_copies)


def factors(ph, q):
    ph_hi, ph_lo = split(ph)
    q_hi, q_lo = split(q)
    return dot(jnp.concatenate([ph_hi, ph_hi, ph_lo], axis=0),
               jnp.concatenate([q_hi, q_lo, q_hi], axis=0), TN)


def weights_kernel(reps, ph, q, w, out):
    approx = factors(ph[0, 0], q[0]) / reps
    out[0] = (w[0, 0].astype(F32) - 0.5 * approx).astype(BF16)


def state_kernel(reps, ph, q, merged, momenta, errors_out, momenta_out):
    approx = factors(ph[0], q[0]) / reps
    errors_out[0] = merged[0] - approx
    momenta_out[0] = 0.9 * momenta[0] + approx


def body(inputs, out_grads, weights, biases, errors, momenta, bias_momenta, q_start):
    L, tok, width = inputs.shape
    G = lax.axis_size("grp")
    R = lax.axis_size("rep")
    rows = width // G
    rank = q_start.shape[2]
    K = L * rank
    Y = G // 2
    scale = float(tok) ** (-0.5)
    pp = -(-K // R)
    pr = -(-K // (G * R))
    chunk = 384 if width % 384 == 0 else 128
    bias_in = jnp.concatenate([bias_momenta, biases.astype(F32)], axis=0)
    vm = pl.BlockSpec(memory_space=pltpu.VMEM)
    hbm = pl.BlockSpec(memory_space=pl.ANY)
    dma = pltpu.SemaphoreType.DMA
    n_rep, n_grp = 1 + 4 * ROUNDS, 2 + 3 * ROUNDS
    merged, phat, q, w_all, bias_sum, small = pl.pallas_call(
        functools.partial(step_kernel, (L, G, R, rank, width, tok, chunk)),
        out_shape=(
            jax.ShapeDtypeStruct((L, rows, width), F32),
            jax.ShapeDtypeStruct((G, K, rows), F32),
            jax.ShapeDtypeStruct((K, width), F32),
            jax.ShapeDtypeStruct((G, L, rows, width), BF16),
            jax.ShapeDtypeStruct((L, width), F32),
            jax.ShapeDtypeStruct((G, 2 * L, rows), F32),
        ),
        in_specs=[hbm, hbm, vm, vm, vm, vm, vm],
        out_specs=(vm, vm, vm, hbm, vm, vm),
        scratch_shapes=[
            pltpu.VMEM((L, tok, width), BF16),
            pltpu.VMEM((L, tok, width), BF16),
            pltpu.VMEM((L, width, width), F32),
            pltpu.VMEM((L, Y, rows, width), BF16),
            pltpu.VMEM((L, Y, rows, width), BF16),
            pltpu.VMEM((L, Y - 1, rows, width), BF16),
            pltpu.VMEM((L, Y - 1, rows, width), BF16),
            pltpu.VMEM((L, rows, width), BF16),
            pltpu.VMEM((L, rows, width), BF16),
            pltpu.VMEM((L, rows, width), BF16),
            pltpu.VMEM((ROUNDS, R, pp, rows), F32),
            pltpu.VMEM((ROUNDS, R, pp, rows), F32),
            pltpu.VMEM((ROUNDS, G, R, pp, rows), F32),
            pltpu.VMEM((ROUNDS, G, R, pr, width), F32),
            pltpu.VMEM((ROUNDS, G, R, pr, width), F32),
            pltpu.VMEM((ROUNDS, R, pr, width), F32),
            pltpu.VMEM((ROUNDS, R, pr, width), F32),
            pltpu.VMEM((ROUNDS, G, R, pr, width), F32),
            pltpu.VMEM((R, L, width), F32),
            pltpu.VMEM((G, L, width), F32),
            pltpu.VMEM((G, 2 * L, rows), F32),
            dma((2 * L + 1,)),
            dma((L,)), dma((L,)),
            dma((L, Y - 1)), dma((L, Y - 1)),
            dma((G - 1,)), dma((G - 1,)),
            dma((n_rep, R - 1)), dma((n_rep, R - 1)),
            dma((n_grp, G - 1)), dma((n_grp, G - 1)),
        ],
        compiler_params=pltpu.CompilerParams(
            collective_id=0, has_side_effects=True, vmem_limit_bytes=62 * 2**20),
        cost_estimate=pl.CostEstimate(
            flops=2 * L * tok * width * width, bytes_accessed=4 * L * tok * width, transcendentals=0),
    )(inputs, out_grads, errors[0], weights, momenta, jnp.swapaxes(q_start, 1, 2), bias_in)

    new_weights = pl.pallas_call(
        functools.partial(weights_kernel, R),
        out_shape=jax.ShapeDtypeStruct((L, width, width), BF16),
        grid=(L, G),
        in_specs=[
            pl.BlockSpec((1, 1, rank, rows), lambda l, g: (g, l, 0, 0)),
            pl.BlockSpec((1, rank, width), lambda l, g: (l, 0, 0)),
            pl.BlockSpec((1, 1, rows, width), lambda l, g: (g, l, 0, 0)),
        ],
        out_specs=pl.BlockSpec((1, rows, width), lambda l, g: (l, g, 0)),
        compiler_params=pltpu.CompilerParams(vmem_limit_bytes=32 * 2**20),
    )(phat.reshape(G, L, rank, rows), q.reshape(L, rank, width), w_all)

    own = lax.dynamic_index_in_dim(phat, lax.axis_index("grp"), 0, keepdims=False)
    block = pl.BlockSpec((1, rows, width), lambda l: (l, 0, 0))
    new_errors, new_momenta = pl.pallas_call(
        functools.partial(state_kernel, R),
        out_shape=(jax.ShapeDtypeStruct((L, rows, width), F32),) * 2,
        grid=(L,),
        in_specs=[
            pl.BlockSpec((1, rank, rows), lambda l: (l, 0, 0)),
            pl.BlockSpec((1, rank, width), lambda l: (l, 0, 0)),
            block, block,
        ],
        out_specs=(block, block),
        compiler_params=pltpu.CompilerParams(vmem_limit_bytes=32 * 2**20),
    )(own.reshape(L, rank, rows), q.reshape(L, rank, width), merged, momenta)

    bias_grad = bias_sum * (scale / R)
    full = jnp.swapaxes(small, 0, 1).reshape(2 * L, width)
    bias_m = 0.9 * full[:L] + bias_grad
    new_biases = (full[L:] - 0.5 * bias_m).astype(BF16)
    new_bias_momenta = lax.dynamic_slice_in_dim(bias_m, lax.axis_index("grp") * rows, rows, 1)
    return (new_weights, new_biases, new_errors[None], new_momenta, new_bias_momenta)


def solution(mesh):
    placed = (
        P(None, ("rep", "grp"), None),
        P(None, ("rep", "grp"), None),
        P(None, "grp", None),
        P(None, "grp"),
        P("rep", None, "grp", None),
        P(None, "grp", None),
        P(None, "grp"),
        P(),
    )
    return jax.shard_map(
        body,
        mesh=mesh,
        in_specs=placed,
        out_specs=(P(), P(), P("rep", None, "grp", None), P(None, "grp", None), P(None, "grp")),
        check_vma=False,
    )
```

```python
import functools

import jax
import jax.numpy as jnp
from jax import lax
from jax.experimental import pallas as pl
from jax.experimental.pallas import tpu as pltpu
from jax.sharding import PartitionSpec as P

ROUNDS = 2
NS_STEPS = 5
F32 = jnp.float32
BF16 = jnp.bfloat16
NN = (((1,), (0,)), ((), ()))
NT = (((1,), (1,)), ((), ()))
TN = (((0,), (0,)), ((), ()))


def dot(a, b, dims, precision=None):
    return lax.dot_general(a, b, dims, precision=precision, preferred_element_type=F32)


def split(a):
    hi = a.astype(BF16)
    return hi, (a - hi.astype(F32)).astype(BF16)


def dot3(a, b):
    a_hi, a_lo = split(a)
    b_hi, b_lo = split(b)
    return dot(jnp.concatenate([a_hi, a_hi, a_lo], axis=1),
               jnp.concatenate([b_hi, b_lo, b_hi], axis=0), NN)


def factors(ph, q):
    ph_hi, ph_lo = split(ph)
    q_hi, q_lo = split(q)
    return dot(jnp.concatenate([ph_hi, ph_hi, ph_lo], axis=0),
               jnp.concatenate([q_hi, q_lo, q_hi], axis=0), TN)


def step_kernel(sizes, x_hbm, y_hbm, errors, weights, momenta, q0, bias_in,
                merged, phat_out, q_out, w_out, bias_out, small_out,
                xbuf, ybuf, gfull, gsend, grecv, ysend, yrecv, mhi, mlo, wown,
                psend, prs, pfull, tsend, trs, tmid, trr, tag, brep, bgrp, bsmall,
                load_sem, s_core, r_core, s_y, r_y, s_wc, r_wc, s_rep, r_rep, s_grp, r_grp):
    L, G, R, rank, width, tok, chunk, pieces = sizes
    rows = width // G
    K = L * rank
    Y = G // 2
    pp = psend.shape[2]
    pr = tsend.shape[3]
    scale = float(tok) ** (-0.5)
    me_r = lax.axis_index("rep")
    me_g = lax.axis_index("grp")
    core = lax.rem(me_g, 2)
    yy = lax.div(me_g, 2)
    mate = me_g + 1 - 2 * core

    loads = []
    for l in range(L):
        for which, (src, dst) in enumerate(((x_hbm, xbuf), (y_hbm, ybuf))):
            loads.append(pltpu.make_async_copy(src.at[l], dst.at[l], load_sem.at[2 * l + which]))
            loads[-1].start()

    barrier = pltpu.get_barrier_semaphore()
    for d in range(1, R):
        pl.semaphore_signal(barrier, inc=1, device_id={"rep": lax.rem(me_r + d, R)},
                            device_id_type=pl.DeviceIdType.MESH)
    for d in range(1, G):
        pl.semaphore_signal(barrier, inc=1, device_id={"grp": lax.rem(me_g + d, G)},
                            device_id_type=pl.DeviceIdType.MESH)
    pl.semaphore_wait(barrier, R + G - 2)

    def remote(src, dst, send, recv, axis, peer):
        copy = pltpu.make_async_remote_copy(
            src_ref=src, dst_ref=dst, send_sem=send, recv_sem=recv,
            device_id={axis: peer}, device_id_type=pl.DeviceIdType.MESH)
        copy.start()
        return copy

    def over_rep(phase, src, dst):
        return [remote(src(lax.rem(me_r + d, R)), dst, s_rep.at[phase, d - 1], r_rep.at[phase, d - 1],
                       "rep", lax.rem(me_r + d, R)) for d in range(1, R)]

    def over_grp(phase, src, dst):
        return [remote(src(lax.rem(me_g + d, G)), dst, s_grp.at[phase, d - 1], r_grp.at[phase, d - 1],
                       "grp", lax.rem(me_g + d, G)) for d in range(1, G)]

    def wait(copies):
        for copy in copies:
            copy.wait_recv()
        for copy in copies:
            copy.wait_send()

    def row_ds(g):
        return pl.ds(pl.multiple_of(g * rows, 16), rows)

    half = lax.rem(me_r, 2)
    pair = me_r + 1 - 2 * half
    hl = L // 2
    first = pl.ds(half * hl, hl)
    second = pl.ds((1 - half) * hl, hl)
    for l in range(L):
        wown[l] = (weights[l].astype(F32) - 0.45 * momenta[l]).astype(BF16)
    w_y = [remote(wown.at[first], w_out.at[me_g, first], s_wc.at[0, d], r_wc.at[0, d], "grp",
                  2 * lax.rem(yy + d, Y) + core) for d in range(1, Y)]
    w_rest = [remote(wown, w_out.at[me_g], s_wc.at[0, 0], r_wc.at[0, 0], "grp", mate)]
    local_w = pltpu.make_async_copy(wown, w_out.at[me_g], load_sem.at[2 * L])
    local_w.start()

    def w_forward():
        copies = []
        for d in range(1, Y):
            w_y[d - 1].wait_recv()
            got = w_out.at[2 * lax.rem(yy + Y - d, Y) + core, first]
            copies.append(remote(got, got, s_wc.at[1, d], r_wc.at[1, d], "rep", pair))
            w_rest.append(remote(got, got, s_wc.at[2, d], r_wc.at[2, d], "grp", mate))
        return copies

    def w_last(copies):
        for d in range(1, Y):
            copies[d - 1].wait_recv()
            got = w_out.at[2 * lax.rem(yy + Y - d, Y) + core, second]
            w_rest.append(remote(got, got, s_wc.at[3, d], r_wc.at[3, d], "grp", mate))

    bsmall[me_g] = bias_in[...]
    small_copies = over_grp(0, lambda g: bsmall.at[me_g], bsmall.at[me_g])

    def grads(u):
        l, at = units[u]
        w = at.size
        if at.start == 0:
            loads[2 * l].wait()
            loads[2 * l + 1].wait()

        def one(j, carry):
            lines = pl.ds(pl.multiple_of(j * chunk, 128), chunk)
            gfull[l, lines, at] = dot(xbuf[l, :, lines], ybuf[l, :, at], TN)
            return carry

        lax.fori_loop(0, width // chunk, one, 0)
        for y in range(Y):
            gsend[l, y, :, at] = gfull[l, row_ds(2 * y + 1 - core), at].astype(BF16)
        return remote(gsend.at[l, :, :, at], grecv.at[l, :, :, at], s_core.at[u], r_core.at[u],
                      "grp", mate)

    def to_y(u):
        l, at = units[u]
        core_copies[u].wait_recv()
        copies = []
        for d in range(1, Y):
            y = lax.rem(yy + d, Y)
            ysend[l, d - 1, :, at] = (gfull[l, row_ds(2 * y + core), at]
                                      + grecv[l, y, :, at].astype(F32)).astype(BF16)
            copies.append(remote(ysend.at[l, d - 1, :, at], yrecv.at[l, d - 1, :, at],
                                 s_y.at[u, d - 1], r_y.at[u, d - 1], "grp", 2 * y + core))
        return copies

    units = [(l, pl.ds(start, size)) for l in range(L) for start, size in pieces]
    core_copies, y_copies = [], []
    for u in range(len(units)):
        core_copies.append(grads(u))
        if u > 0:
            y_copies.append(to_y(u - 1))
    y_copies.append(to_y(len(units) - 1))
    for l in range(L):
        total = dot(jnp.ones((8, tok), BF16), ybuf[l], NN)
        brep[me_r, pl.ds(l, 1), :] = total[:1]
    bias_copies = over_rep(0, lambda r: brep.at[me_r], brep.at[me_r])
    w_x = w_forward()
    wait(bias_copies)
    bgrp[me_g] = jnp.sum(brep[...], axis=0)
    bias_copies = over_grp(1, lambda g: bgrp.at[me_g], bgrp.at[me_g])
    for u, (l, at) in enumerate(units):
        for copy in y_copies[u]:
            copy.wait_recv()
        total = gfull[l, row_ds(me_g), at] + grecv[l, yy, :, at].astype(F32)
        for d in range(1, Y):
            total = total + yrecv[l, d - 1, :, at].astype(F32)
        m = total * scale + errors[l, :, at]
        merged[l, :, at] = m
        hi, lo = split(m)
        mhi[l, :, at] = hi
        mlo[l, :, at] = lo

    def apply(a, l, dims):
        hi, lo = split(a)
        both = dot(jnp.concatenate([hi, lo], axis=0), mhi[l], dims)
        return both[:rank] + both[rank:] + dot(hi, mlo[l], dims)

    row = lax.broadcasted_iota(jnp.int32, (K, K), 0)
    col = lax.broadcasted_iota(jnp.int32, (K, K), 1)
    same = (lax.div(row, rank) == lax.div(col, rank)).astype(F32)
    eye = (row == col).astype(F32)
    layer_of = lax.div(lax.broadcasted_iota(jnp.int32, (K, 1), 0), rank)

    q = [q0[l] for l in range(L)]
    for rnd in range(ROUNDS):
        p = jnp.concatenate([apply(q[l], l, NT) for l in range(L)], axis=0)
        for r in range(R):
            if r * pp < K:
                psend[rnd, r] = p[r * pp:(r + 1) * pp]
        prs[rnd, me_r] = psend[rnd, me_r]
        wait(over_rep(1 + 4 * rnd, lambda r: psend.at[rnd, r], prs.at[rnd, me_r]))
        pfull[rnd, me_g, me_r] = jnp.sum(prs[rnd], axis=0)
        wait(over_rep(2 + 4 * rnd, lambda r: pfull.at[rnd, me_g, me_r], pfull.at[rnd, me_g, me_r]))
        p_copies = over_grp(2 + 3 * rnd, lambda g: pfull.at[rnd, me_g], pfull.at[rnd, me_g])

        def whole_p(g):
            return jnp.concatenate([pfull[rnd, g, r] for r in range(R)], axis=0)[:K]

        p = whole_p(me_g)
        t = jnp.concatenate([apply(p[l * rank:(l + 1) * rank], l, NN) for l in range(L)], axis=0)
        for i in range(G * R):
            if i * pr < K:
                tsend[rnd, i // R, i % R] = t[i * pr:(i + 1) * pr]
        trs[rnd, me_g] = tsend[rnd, me_g]
        copies = over_grp(3 + 3 * rnd, lambda g: tsend.at[rnd, g], trs.at[rnd, me_g])

        wait(p_copies)
        gram = jnp.zeros((K, K), F32)
        for g in range(G):
            pg = whole_p(g)
            hi, lo = split(pg)
            both = jnp.concatenate([hi, lo], axis=0)
            both = dot(both, both, NT)
            gram = gram + (both[:K, :K] + both[:K, K:] + both[K:, :K])
        gram = gram * same
        squares = jnp.sum(gram * gram, axis=1, keepdims=True)
        fro = jnp.zeros((K, 1), F32)
        for l in range(L):
            mine = layer_of == l
            one = jnp.sum(jnp.where(mine, squares, 0.0), axis=0, keepdims=True)
            fro = jnp.where(mine, jnp.sqrt(one) + 1e-06, fro)
        ymat, zmat = gram / fro, eye

        def newton(ymat, zmat, count):
            for _ in range(count):
                tmat = 1.5 * eye - 0.5 * dot3(zmat, ymat)
                ymat = dot3(ymat, tmat)
                zmat = dot3(tmat, zmat)
            return ymat, zmat

        if rnd == 0:
            w_last(w_x)
        ymat, zmat = newton(ymat, zmat, 1)
        wait(copies)
        tmid[rnd] = jnp.sum(trs[rnd], axis=0)
        trr[rnd, me_r] = tmid[rnd, me_r]
        copies = over_rep(3 + 4 * rnd, lambda r: tmid.at[rnd, r], trr.at[rnd, me_r])
        ymat, zmat = newton(ymat, zmat, 2)
        wait(copies)
        tag[rnd, me_g, me_r] = jnp.sum(trr[rnd], axis=0)
        copies = over_rep(4 + 4 * rnd, lambda r: tag.at[rnd, me_g, me_r], tag.at[rnd, me_g, me_r])
        ymat, zmat = newton(ymat, zmat, NS_STEPS - 3)
        wait(copies)
        wait(over_grp(4 + 3 * rnd, lambda g: tag.at[rnd, me_g], tag.at[rnd, me_g]))
        t = jnp.concatenate([tag[rnd, i // R, i % R] for i in range(G * R)], axis=0)[:K]
        inv = 1.0 / jnp.sqrt(fro)
        qall = factors(zmat, t) * inv
        q = [qall[l * rank:(l + 1) * rank] for l in range(L)]
        if rnd == ROUNDS - 1:
            q_out[...] = qall
            for g in range(G):
                phat_out[g] = factors(zmat, whole_p(g)) * inv

    wait(bias_copies)
    wait(small_copies)
    bias_out[...] = jnp.sum(bgrp[...], axis=0)
    small_out[...] = bsmall[...]
    for u in range(len(units)):
        core_copies[u].wait_send()
        for copy in y_copies[u]:
            copy.wait_send()
    local_w.wait()
    for copy in w_y + w_x:
        copy.wait_send()
    wait(w_rest)


def weights_kernel(reps, ph, q, w, out):
    approx = factors(ph[0, 0], q[0]) / reps
    out[0] = (w[0, 0].astype(F32) - 0.5 * approx).astype(BF16)


def state_kernel(reps, ph, q, merged, momenta, errors_out, momenta_out):
    approx = factors(ph[0], q[0]) / reps
    errors_out[0] = merged[0] - approx
    momenta_out[0] = 0.9 * momenta[0] + approx


def body(inputs, out_grads, weights, biases, errors, momenta, bias_momenta, q_start):
    L, tok, width = inputs.shape
    G = lax.axis_size("grp")
    R = lax.axis_size("rep")
    rows = width // G
    rank = q_start.shape[2]
    K = L * rank
    Y = G // 2
    scale = float(tok) ** (-0.5)
    pp = -(-K // R)
    pr = -(-K // (G * R))
    chunk = 384 if width % 384 == 0 else 128
    cut = width // 256 // 2 * 256
    pieces = ((0, cut), (cut, width - cut))
    bias_in = jnp.concatenate([bias_momenta, biases.astype(F32)], axis=0)
    vm = pl.BlockSpec(memory_space=pltpu.VMEM)
    hbm = pl.BlockSpec(memory_space=pl.ANY)
    dma = pltpu.SemaphoreType.DMA
    n_rep, n_grp = 1 + 4 * ROUNDS, 2 + 3 * ROUNDS
    merged, phat, q, w_all, bias_sum, small = pl.pallas_call(
        functools.partial(step_kernel, (L, G, R, rank, width, tok, chunk, pieces)),
        out_shape=(
            jax.ShapeDtypeStruct((L, rows, width), F32),
            jax.ShapeDtypeStruct((G, K, rows), F32),
            jax.ShapeDtypeStruct((K, width), F32),
            jax.ShapeDtypeStruct((G, L, rows, width), BF16),
            jax.ShapeDtypeStruct((L, width), F32),
            jax.ShapeDtypeStruct((G, 2 * L, rows), F32),
        ),
        in_specs=[hbm, hbm, vm, vm, vm, vm, vm],
        out_specs=(vm, vm, vm, hbm, vm, vm),
        scratch_shapes=[
            pltpu.VMEM((L, tok, width), BF16),
            pltpu.VMEM((L, tok, width), BF16),
            pltpu.VMEM((L, width, width), F32),
            pltpu.VMEM((L, Y, rows, width), BF16),
            pltpu.VMEM((L, Y, rows, width), BF16),
            pltpu.VMEM((L, Y - 1, rows, width), BF16),
            pltpu.VMEM((L, Y - 1, rows, width), BF16),
            pltpu.VMEM((L, rows, width), BF16),
            pltpu.VMEM((L, rows, width), BF16),
            pltpu.VMEM((L, rows, width), BF16),
            pltpu.VMEM((ROUNDS, R, pp, rows), F32),
            pltpu.VMEM((ROUNDS, R, pp, rows), F32),
            pltpu.VMEM((ROUNDS, G, R, pp, rows), F32),
            pltpu.VMEM((ROUNDS, G, R, pr, width), F32),
            pltpu.VMEM((ROUNDS, G, R, pr, width), F32),
            pltpu.VMEM((ROUNDS, R, pr, width), F32),
            pltpu.VMEM((ROUNDS, R, pr, width), F32),
            pltpu.VMEM((ROUNDS, G, R, pr, width), F32),
            pltpu.VMEM((R, L, width), F32),
            pltpu.VMEM((G, L, width), F32),
            pltpu.VMEM((G, 2 * L, rows), F32),
            dma((2 * L + 1,)),
            dma((2 * L,)), dma((2 * L,)),
            dma((2 * L, Y - 1)), dma((2 * L, Y - 1)),
            dma((4, Y)), dma((4, Y)),
            dma((n_rep, R - 1)), dma((n_rep, R - 1)),
            dma((n_grp, G - 1)), dma((n_grp, G - 1)),
        ],
        compiler_params=pltpu.CompilerParams(
            collective_id=0, has_side_effects=True, vmem_limit_bytes=62 * 2**20),
        cost_estimate=pl.CostEstimate(
            flops=2 * L * tok * width * width, bytes_accessed=4 * L * tok * width, transcendentals=0),
    )(inputs, out_grads, errors[0], weights, momenta, jnp.swapaxes(q_start, 1, 2), bias_in)

    new_weights = pl.pallas_call(
        functools.partial(weights_kernel, R),
        out_shape=jax.ShapeDtypeStruct((L, width, width), BF16),
        grid=(L, G),
        in_specs=[
            pl.BlockSpec((1, 1, rank, rows), lambda l, g: (g, l, 0, 0)),
            pl.BlockSpec((1, rank, width), lambda l, g: (l, 0, 0)),
            pl.BlockSpec((1, 1, rows, width), lambda l, g: (g, l, 0, 0)),
        ],
        out_specs=pl.BlockSpec((1, rows, width), lambda l, g: (l, g, 0)),
        compiler_params=pltpu.CompilerParams(vmem_limit_bytes=32 * 2**20),
    )(phat.reshape(G, L, rank, rows), q.reshape(L, rank, width), w_all)

    own = lax.dynamic_index_in_dim(phat, lax.axis_index("grp"), 0, keepdims=False)
    block = pl.BlockSpec((1, rows, width), lambda l: (l, 0, 0))
    new_errors, new_momenta = pl.pallas_call(
        functools.partial(state_kernel, R),
        out_shape=(jax.ShapeDtypeStruct((L, rows, width), F32),) * 2,
        grid=(L,),
        in_specs=[
            pl.BlockSpec((1, rank, rows), lambda l: (l, 0, 0)),
            pl.BlockSpec((1, rank, width), lambda l: (l, 0, 0)),
            block, block,
        ],
        out_specs=(block, block),
        compiler_params=pltpu.CompilerParams(vmem_limit_bytes=32 * 2**20),
    )(own.reshape(L, rank, rows), q.reshape(L, rank, width), merged, momenta)

    bias_grad = bias_sum * (scale / R)
    full = jnp.swapaxes(small, 0, 1).reshape(2 * L, width)
    bias_m = 0.9 * full[:L] + bias_grad
    new_biases = (full[L:] - 0.5 * bias_m).astype(BF16)
    new_bias_momenta = lax.dynamic_slice_in_dim(bias_m, lax.axis_index("grp") * rows, rows, 1)
    return (new_weights, new_biases, new_errors[None], new_momenta, new_bias_momenta)


def solution(mesh):
    placed = (
        P(None, ("rep", "grp"), None),
        P(None, ("rep", "grp"), None),
        P(None, "grp", None),
        P(None, "grp"),
        P("rep", None, "grp", None),
        P(None, "grp", None),
        P(None, "grp"),
        P(),
    )
    return jax.shard_map(
        body,
        mesh=mesh,
        in_specs=placed,
        out_specs=(P(), P(), P("rep", None, "grp", None), P(None, "grp", None), P(None, "grp")),
        check_vma=False,
    )
```
